256 devices in a mesh: ctx: 32 (over z, x), head: 8 (over y, core).
Axes of the slice: x: 4, y: 4, z: 8, core: 2. Of those that a mesh axis runs over, the one named last changes fastest.
Arguments:
- query: bfloat16 [32768, 4096], P(('ctx', 'head')), may hold values from -90 to 90
- keys: bfloat16 [32768, 4096], P(('ctx', 'head')), may hold values from -4.5 to 4.5
- values: bfloat16 [32768, 4096], P(('ctx', 'head')), may hold values from -5 to 5
- grad_out: bfloat16 [32768, 4096], P(('ctx', 'head')), may hold values from -5 to 5
- random_owner: int32 [256, 3], replicated, may hold values from 0 to 31, all different within a row; in each aligned block of 8 rows (0 to 7, 8 to 15, ...) no two rows name the same one
- random_within: int32 [256, 3], replicated, may hold values from 0 to 7
- global_ids: int32 [256, 2], replicated, may hold values from 0 to 3, all different within a row
Outputs:
- grad_query: bfloat16 [32768, 4096], P(('ctx', 'head'))
- grad_keys: bfloat16 [32768, 4096], P(('ctx', 'head'))
- grad_values: bfloat16 [32768, 4096], P(('ctx', 'head'))
The draws below stay inside these ranges and needn't reach their ends.
Inputs may be any that keep to these rules, and one draw needn't show every extreme that they name: `random_owner`: in the 8 rows of one index of ctx no owner is named more than 1 times, a bound that some block reaches in some of them; the 3 owners of one row differ. `global_ids`: the 2 blocks of one row differ; every block 0 to 3 is named by some row.
All inputs are finite; a program needn't handle non-finite values.
Results may differ from the reference program's by a relative error of at most 0.0053.
Values may be sent and summed in bfloat16 or wider, within the bound.
No kernel may reach another device: no remote copies, remote signals or barrier semaphores. Data moves between devices by JAX's collectives and lax.ppermute only.
A program may use at most 192 MiB of HBM per device.

```python
import math
import jax
import jax.numpy as jnp
import numpy as np
from jax import lax

HEADS = 32
HEAD_DIM = 128
BLOCK = 128
BPD = 8
RAND = 3
GLOB = 2
NGLOB = 4
CAP = 1
QBLOCKS = 256
SEQ = 32768
N_CTX = 32


def draw_pair(key):
    base_key = jax.random.fold_in(key, 11)
    key_keys, key_query = jax.random.split(base_key, 2)
    full_shape = (SEQ, HEADS * HEAD_DIM)
    keys_draw = jnp.clip(jax.random.normal(key_keys, full_shape, jnp.float32), -4.5, 4.5)
    query_draw = jnp.clip(jax.random.normal(key_query, full_shape, jnp.float32), -4.5, 4.5)
    return (query_draw, keys_draw)


def draw_query(key, part):
    return draw_pair(key)[0].astype(jnp.bfloat16)


def draw_keys(key, part):
    return draw_pair(key)[1].astype(jnp.bfloat16)


def touch_ends(drawn, key, low, high):
    longest = drawn.shape.index(max(drawn.shape))
    spots = []
    for shift in (0, 1):
        where = [jax.random.randint(jax.random.fold_in(key, axis), (), 0, length) for axis, length in enumerate(drawn.shape)]
        where[longest] = (where[longest] + shift) % drawn.shape[longest]
        spots.append(tuple(where))
    return drawn.at[spots[0]].set(low).at[spots[1]].set(high)


def steps_of(own_key, extent, pieces, least, top_value):
    def one(dim, blocks):
        heights = jax.random.uniform(jax.random.fold_in(jax.random.fold_in(own_key, 6), dim), (blocks,), jnp.float32, least / len(pieces), top_value / len(pieces))
        return jnp.repeat(jnp.exp(heights), extent[dim] // blocks).reshape((-1,) + (1,) * (len(extent) - dim - 1))

    level = one(*pieces[0])
    for cut in pieces[1:]:
        level = level * one(*cut)
    return level


def choose_distinct(stream_key, rows, count, top, lift):
    order = jax.random.permutation(jax.random.fold_in(stream_key, 1), count)
    favour = order
    for power in range(3):
        favour = favour * favour // count
    favour = favour * lift // count
    lots = jax.random.randint(jax.random.fold_in(stream_key, 2), (rows, count), 0, 4096) + favour
    fixed_rows = jax.random.permutation(jax.random.fold_in(stream_key, 3), rows)[jnp.arange(count) % rows]
    lots = jnp.where(jnp.arange(rows)[:, None] == fixed_rows[None, :], 1 << 14, lots)
    priority = lots * count + jnp.arange(count)
    return lax.top_k(priority.astype(jnp.int32), top)[1].astype(jnp.int32)


def deal_out(stream_key, own, number, rows, count, top, most, slope):
    sequence = jax.random.permutation(stream_key, count)
    crowded, usual = shares(count, rows * top, most, slope, True), shares(count, rows * top, most, slope, False)
    places = jnp.arange(count)

    def named(tallies, offset_by):
        used = int((tallies > 0).sum())
        fixed = max(1, used // 4)
        moved = fixed + (places - fixed + offset_by * (used - fixed)) % max(1, count - fixed)
        return jnp.zeros((count,), jnp.int32).at[sequence[jnp.where(places < fixed, places, moved)]].set(jnp.asarray(tallies, jnp.int32))

    tallies = jnp.where(number % 4 == 0, named(crowded, number // 4), named(usual, number - number // 4 - 1))
    mixed = jax.random.permutation(jax.random.fold_in(own, 3), count)
    giver, sink = mixed[0:count // 2 * 2:2], mixed[1:count // 2 * 2:2]
    margin = jnp.minimum(tallies[giver] - 1, most - tallies[sink]) // 2
    margin = jnp.where((giver == sequence[0]) | (sink == sequence[0]) | (tallies[sink] == 0), 0, jnp.maximum(margin, 0))
    moved = jax.random.randint(jax.random.fold_in(own, 4), (count // 2,), 0, 1 << 20) % (margin + 1)
    tallies = tallies.at[giver].add(-moved).at[sink].add(moved)
    items = jnp.searchsorted(jnp.cumsum(tallies), jnp.arange(rows * top), side="right").astype(jnp.int32)
    table = items.reshape(top, rows).T
    table = table[jax.random.permutation(jax.random.fold_in(own, 1), rows)]
    offset_by = jax.random.randint(jax.random.fold_in(own, 2), (rows, 1), 0, top)
    return jnp.take_along_axis(table, (jnp.arange(top)[None, :] + offset_by) % top, axis=1)


def shares(amount, total, most, slope, full):
    loads = [(1 << 20) // math.isqrt(grade ** slope) + 1 for grade in range(1, amount + 1)]
    largest = most if full else min(most, max(-(-total // amount), total * loads[0] // sum(loads)))
    least = 1 if total - largest >= amount - 1 else 0
    given, spare = [largest] + [least] * (amount - 1), total - largest - least * (amount - 1)
    while spare > 0:
        movable = [i for i in range(1, amount) if given[i] < largest] or [i for i in range(1, amount) if given[i] < most]
        mass, left = sum([loads[i] for i in movable]), spare
        for i in movable:
            more = min(most - given[i], max(1, left * loads[i] // mass), spare)
            given[i] = given[i] + more
            spare = spare - more
    return np.array(given)


def scatter_about(rng, extent, deviation, most, cuts=(), held_as=jnp.bfloat16):
    entries = jax.random.normal(rng, extent, jnp.float32) * deviation
    if len(cuts) > 0:
        entries = steps_of(rng, extent, cuts, -0.22, 0.18) * entries
    return jnp.clip(entries, min=-most, max=most).astype(held_as)


def setup_inputs(seed: int = 0) -> dict:
    streams_of = jax.random.split(jax.random.key(seed), 8)
    query = draw_query(jax.random.fold_in(streams_of[7], 71), 0)
    keys = draw_keys(jax.random.fold_in(streams_of[7], 71), 0)
    values = scatter_about(streams_of[2], (SEQ, HEADS * HEAD_DIM), 1.0, 5.0, ((0, 256),))
    grad_out = scatter_about(streams_of[3], (SEQ, HEADS * HEAD_DIM), 1.0, 5.0, ((0, 256),))
    random_owner_keys = jax.random.split(jax.random.fold_in(streams_of[4], 1), QBLOCKS // BPD)
    random_owner_turns = jax.random.permutation(jax.random.fold_in(streams_of[4], 3), QBLOCKS // BPD)
    random_owner = jax.vmap(lambda own, number: deal_out(jax.random.fold_in(streams_of[4], 2), own, number, BPD, N_CTX, RAND, CAP, 2))(random_owner_keys, random_owner_turns).reshape((QBLOCKS, RAND))
    random_within = touch_ends(jax.random.randint(streams_of[5], (QBLOCKS, RAND), 0, BPD), jax.random.fold_in(streams_of[5], 1), 0, BPD - 1).astype(jnp.int32)
    global_ids = choose_distinct(streams_of[6], QBLOCKS, NGLOB, GLOB, 4096)
    return {"query": query, "keys": keys, "values": values, "grad_out": grad_out, "random_owner": random_owner, "random_within": random_within, "global_ids": global_ids}


def reference(query, keys, values, grad_out, random_owner, random_within, global_ids):
    blocks = SEQ // BLOCK
    score_scale = HEAD_DIM ** -0.5
    block_shape = (blocks, BLOCK, HEADS, HEAD_DIM)
    query_blocks = query.reshape(block_shape)
    key_blocks = keys.reshape(block_shape)
    value_blocks = values.reshape(block_shape)
    grad_blocks = grad_out.reshape(block_shape)
    indices = jnp.arange(blocks, dtype=jnp.int32)
    random_ids = (random_owner * BPD + random_within).astype(jnp.int32)
    key_lists = jnp.concatenate([(indices - 1)[:, None], indices[:, None], (indices + 1)[:, None], global_ids.astype(jnp.int32), random_ids], axis=1)
    list_valid = (key_lists >= 0) & (key_lists < blocks)
    safe_lists = jnp.clip(key_lists, 0, blocks - 1).astype(jnp.int32)
    slot_random = jnp.arange(3 + GLOB + RAND) >= 3 + GLOB

    def one_block(carried, index):
        sum_keys, sum_values = carried
        key_ids = safe_lists[index]
        slot_ok = list_valid[index]
        query_f = query_blocks[index].astype(jnp.float32)
        grad_f = grad_blocks[index].astype(jnp.float32)
        keys_f = key_blocks[key_ids].astype(jnp.float32)
        values_f = value_blocks[key_ids].astype(jnp.float32)
        scores = jnp.einsum("qhd,nkhd->hqnk", query_f, keys_f) * score_scale
        scores = jnp.where(slot_ok[None, None, :, None], scores, -jnp.inf)
        highest = jnp.max(scores, axis=(2, 3), keepdims=True)
        logsum = highest + jnp.log(jnp.sum(jnp.exp(scores - highest), axis=(2, 3), keepdims=True))
        probs = jnp.exp(scores - logsum)
        probs_low = lax.optimization_barrier(probs.astype(jnp.bfloat16)).astype(jnp.float32)
        dprobs = jnp.einsum("qhd,nkhd->hqnk", grad_f, values_f)
        row_dot = jnp.sum(probs * dprobs, axis=(2, 3), keepdims=True)
        dscores = lax.optimization_barrier((probs * (dprobs - row_dot)).astype(jnp.bfloat16)).astype(jnp.float32)
        grad_query = jnp.einsum("hqnk,nkhd->qhd", dscores, keys_f) * score_scale
        key_terms = jnp.einsum("hqnk,qhd->nkhd", dscores, query_f) * score_scale
        value_terms = jnp.einsum("hqnk,qhd->nkhd", probs_low, grad_f)
        key_rounded = lax.optimization_barrier(key_terms.astype(jnp.bfloat16)).astype(jnp.float32)
        value_rounded = lax.optimization_barrier(value_terms.astype(jnp.bfloat16)).astype(jnp.float32)
        key_terms = jnp.where(slot_random[:, None, None, None], key_rounded, key_terms)
        value_terms = jnp.where(slot_random[:, None, None, None], value_rounded, value_terms)
        sum_keys = sum_keys.at[key_ids].add(key_terms)
        sum_values = sum_values.at[key_ids].add(value_terms)
        return (sum_keys, sum_values), grad_query.astype(jnp.bfloat16)

    zero_sums = jnp.zeros(block_shape, jnp.float32)
    finals, grad_queries = lax.scan(one_block, (zero_sums, zero_sums), indices)
    grad_query = grad_queries.reshape(SEQ, HEADS * HEAD_DIM)
    grad_keys = finals[0].reshape(SEQ, HEADS * HEAD_DIM).astype(jnp.bfloat16)
    grad_values = finals[1].reshape(SEQ, HEADS * HEAD_DIM).astype(jnp.bfloat16)
    return (grad_query, grad_keys, grad_values)
```

```python
from functools import partial

import jax
import jax.numpy as jnp
from jax import lax
from jax.experimental import pallas as pl
from jax.experimental.pallas import tpu as pltpu
from jax.sharding import Mesh, PartitionSpec as P

HEAD_DIM = 128
BLOCK = 128
RAND = 3
GLOB = 2
NGLOB = 4
NX = 4
SLOTS = 3 + GLOB
BF16 = jnp.bfloat16
F32 = jnp.float32
VMEM_LIMIT = 58 * 1024 * 1024
SCALE = HEAD_DIM ** (-0.5)
CTX = ("z", "x")


def dot_nt(a, b):
    return lax.dot_general(a, b, (((1,), (1,)), ((), ())), preferred_element_type=F32)


def dot_nn(a, b):
    return lax.dot_general(a, b, (((1,), (0,)), ((), ())), preferred_element_type=F32)


def dot_tn(a, b):
    return lax.dot_general(a, b, (((0,), (0,)), ((), ())), preferred_element_type=F32)


def params():
    return pltpu.CompilerParams(vmem_limit_bytes=VMEM_LIMIT)


def whole(shape):
    return pl.BlockSpec(shape, lambda *_: (0,) * len(shape))


def call(body, grid, scalars, ins, in_specs, out_shape, out_specs, scratch=()):
    return pl.pallas_call(
        body,
        grid_spec=pltpu.PrefetchScalarGridSpec(
            num_scalar_prefetch=len(scalars),
            grid=grid,
            in_specs=in_specs,
            out_specs=out_specs,
            scratch_shapes=list(scratch),
        ),
        out_shape=out_shape,
        compiler_params=params(),
    )(*scalars, *ins)


def pick_body(row_ref, x_ref, o_ref):
    o_ref[0] = x_ref[row_ref[pl.program_id(0)]]


def pick_rows(rows_of, x, count):
    block = (1,) + x.shape[1:]
    zeros = (0,) * (x.ndim - 1)
    return call(
        pick_body,
        (count,),
        (rows_of,),
        (x,),
        [whole(x.shape)],
        jax.ShapeDtypeStruct((count,) + x.shape[1:], x.dtype),
        pl.BlockSpec(block, lambda i, *_: (i,) + zeros),
    )


def order_body(count, place_ref, *refs):
    out = refs[count]
    for s in range(count):
        out[place_ref[s]] = refs[s][...]


def put_in_order(places, pieces):
    count = len(pieces)
    shape = pieces[0].shape
    return call(
        partial(order_body, count),
        (1,),
        (places,),
        pieces,
        [whole(shape)] * count,
        jax.ShapeDtypeStruct((count,) + shape, pieces[0].dtype),
        whole((count,) + shape),
    )


def extend_body(rows, place_ref, kv_ref, left_ref, right_ref, *refs):
    out = refs[NGLOB]
    out[0] = left_ref[...]
    for r in range(rows):
        out[1 + r] = kv_ref[r]
    out[rows + 1] = right_ref[...]
    for s in range(NGLOB):
        out[rows + 2 + place_ref[s]] = refs[s][...]


def extend(places, kv_rows, left, right, summary):
    rows = kv_rows.shape[0]
    shape = left.shape
    full = (rows + 2 + NGLOB,) + shape
    return call(
        partial(extend_body, rows),
        (1,),
        (places,),
        (kv_rows, left, right, *summary),
        [whole(kv_rows.shape)] + [whole(shape)] * (2 + NGLOB),
        jax.ShapeDtypeStruct(full, kv_rows.dtype),
        whole(full),
    )


def local_scores(slot_ref, edge_ref, row, rows, kv_ref, q, h):
    cols = slice(h * HEAD_DIM, (h + 1) * HEAD_DIM)
    parts = []
    for j in range(SLOTS):
        s = dot_nt(kv_ref[slot_ref[row * SLOTS + j], 0, :, cols], q) * SCALE
        if j == 0:
            s = jnp.where((row == 0) & (edge_ref[0] != 0), -jnp.inf, s)
        if j == 2:
            s = jnp.where((row == rows - 1) & (edge_ref[1] != 0), -jnp.inf, s)
        parts.append(s)
    return parts


def local_stats_body(rows, heads, slot_ref, edge_ref, x_ref, kv_ref, o_ref):
    row = pl.program_id(0)
    for h in range(heads):
        cols = slice(h * HEAD_DIM, (h + 1) * HEAD_DIM)
        q = x_ref[0, 0, :, cols]
        g = x_ref[0, 1, :, cols]
        scores = local_scores(slot_ref, edge_ref, row, rows, kv_ref, q, h)
        top = jnp.max(scores[0], axis=0, keepdims=True)
        for s in scores[1:]:
            top = jnp.maximum(top, jnp.max(s, axis=0, keepdims=True))
        total = jnp.zeros_like(top)
        mean = jnp.zeros_like(top)
        for j in range(SLOTS):
            p = jnp.exp(scores[j] - top)
            dp = dot_nt(kv_ref[slot_ref[row * SLOTS + j], 1, :, cols], g)
            total += jnp.sum(p, axis=0, keepdims=True)
            mean += jnp.sum(p * dp, axis=0, keepdims=True)
        o_ref[0, h : h + 1, :] = top + jnp.log(total)
        o_ref[0, heads + h : heads + h + 1, :] = mean / total


def entry_stats_body(heads, own_ref, valid_ref, x_ref, kv_ref, o_ref):
    e = pl.program_id(0)
    own = own_ref[e] + 1

    @pl.when(valid_ref[e] != 0)
    def _():
        for h in range(heads):
            cols = slice(h * HEAD_DIM, (h + 1) * HEAD_DIM)
            s = dot_nt(kv_ref[own, 0, :, cols], x_ref[0, 0, :, cols]) * SCALE
            dp = dot_nt(kv_ref[own, 1, :, cols], x_ref[0, 1, :, cols])
            top = jnp.max(s, axis=0, keepdims=True)
            p = jnp.exp(s - top)
            total = jnp.sum(p, axis=0, keepdims=True)
            o_ref[0, h : h + 1, :] = top + jnp.log(total)
            o_ref[0, heads + h : heads + h + 1, :] = jnp.sum(p * dp, axis=0, keepdims=True) / total

    @pl.when(valid_ref[e] == 0)
    def _():
        o_ref[...] = jnp.zeros_like(o_ref)


def place_of(e, nz):
    return (e % NX) * nz + e // NX


def combine_body(rows, heads, count, nz, owner_ref, row_ref, loc_ref, rem_ref, ld_ref, out_ref):
    for r in range(rows):
        parts = [loc_ref[r]]
        for j in range(RAND):
            o = owner_ref[r * RAND + j]
            parts.append(rem_ref[place_of(o, nz)])
        logs = [p[:heads] for p in parts]
        means = [p[heads:] for p in parts]
        top = jnp.maximum(jnp.maximum(logs[0], logs[1]), jnp.maximum(logs[2], logs[3]))
        weights = [jnp.exp(x - top) for x in logs]
        total = sum(weights[1:], weights[0])
        mean = sum([w * m for w, m in zip(weights[1:], means[1:])], weights[0] * means[0])
        ld_ref[r, :heads] = top + jnp.log(total)
        ld_ref[r, heads:] = mean / total
    for o in range(count):
        out_ref[place_of(o, nz)] = ld_ref[row_ref[o]]


def entry_grads_body(
    heads, own_ref, valid_ref, x_ref, ld_ref, kv_ref, dq_ref, acc_ref
):
    e = pl.program_id(0)
    own = own_ref[e]

    @pl.when(e == 0)
    def _():
        acc_ref[...] = jnp.zeros_like(acc_ref)

    @pl.when(valid_ref[e] != 0)
    def _():
        for h in range(heads):
            cols = slice(h * HEAD_DIM, (h + 1) * HEAD_DIM)
            q = x_ref[0, 0, :, cols]
            g = x_ref[0, 1, :, cols]
            k = kv_ref[own + 1, 0, :, cols]
            v = kv_ref[own + 1, 1, :, cols]
            p = jnp.exp(dot_nt(k, q) * SCALE - ld_ref[0, h : h + 1, :])
            dp = dot_nt(v, g)
            ds = (p * (dp - ld_ref[0, heads + h : heads + h + 1, :])).astype(BF16)
            acc_ref[own, 0, :, cols] += dot_nn(ds, q)
            acc_ref[own, 1, :, cols] += dot_nn(p.astype(BF16), g)
            dq_ref[0, :, cols] = (dot_tn(ds, k) * SCALE).astype(BF16)

    @pl.when(valid_ref[e] == 0)
    def _():
        dq_ref[...] = jnp.zeros_like(dq_ref)


def local_grads_body(
    rows, heads, slot_ref, edge_ref, x_ref, ld_ref, kv_ref, dq_ref, rows_ref, side_ref, acc_ref
):
    row = pl.program_id(0)

    @pl.when(row == 0)
    def _():
        acc_ref[...] = jnp.zeros_like(acc_ref)

    for h in range(heads):
        cols = slice(h * HEAD_DIM, (h + 1) * HEAD_DIM)
        q = x_ref[0, 0, :, cols]
        g = x_ref[0, 1, :, cols]
        log = ld_ref[0, h : h + 1, :]
        mean = ld_ref[0, heads + h : heads + h + 1, :]
        scores = local_scores(slot_ref, edge_ref, row, rows, kv_ref, q, h)
        dq = jnp.zeros((BLOCK, HEAD_DIM), F32)
        for j in range(SLOTS):
            slot = slot_ref[row * SLOTS + j]
            p = jnp.exp(scores[j] - log)
            dp = dot_nt(kv_ref[slot, 1, :, cols], g)
            ds = (p * (dp - mean)).astype(BF16)
            acc_ref[slot, 0, :, cols] += dot_nn(ds, q)
            acc_ref[slot, 1, :, cols] += dot_nn(p.astype(BF16), g)
            dq += dot_tn(ds, kv_ref[slot, 0, :, cols])
        dq_ref[0, :, cols] = dq * SCALE

    @pl.when(row == rows - 1)
    def _():
        sources = [0, rows + 1] + [rows + 2 + s for s in range(NGLOB)]
        for place, source in enumerate(sources):
            side_ref[place, 0] = (acc_ref[source, 0] * SCALE).astype(BF16)
            side_ref[place, 1] = acc_ref[source, 1].astype(BF16)
        for r in range(rows):
            rows_ref[r] = acc_ref[1 + r]


def finish_kv_body(
    rows, first_ref, loc_ref, rand_ref, left_ref, right_ref, s0_ref, s1_ref, s2_ref, s3_ref, o_ref
):
    row = pl.program_id(0)
    both = loc_ref[0] + rand_ref[0]
    o = [both[0] * SCALE, both[1]]
    at_first = (row == 0).astype(F32)
    at_last = (row == rows - 1).astype(F32)
    for t in range(2):
        total = o[t] + at_first * left_ref[t].astype(F32) + at_last * right_ref[t].astype(F32)
        for g, s_ref in enumerate((s0_ref, s1_ref, s2_ref, s3_ref)):
            here = ((row == g) & (first_ref[0] != 0)).astype(F32)
            total += here * s_ref[t].astype(F32)
        o_ref[0, t] = total.astype(BF16)


def finish_q_body(owner_ref, loc_ref, a_ref, b_ref, c_ref, o_ref):
    o_ref[0] = (
        loc_ref[0] + a_ref[0].astype(F32) + b_ref[0].astype(F32) + c_ref[0].astype(F32)
    ).astype(BF16)


def exchange_small(x):
    nz = lax.axis_size("z")
    x = x.reshape((NX, nz) + x.shape[1:])
    x = lax.all_to_all(x, "x", split_axis=0, concat_axis=0, tiled=True)
    x = lax.all_to_all(x, "z", split_axis=1, concat_axis=1, tiled=True)
    return x.reshape((NX * nz,) + x.shape[2:])


def ring(axis, shift):
    count = lax.axis_size(axis)
    return [(i, (i + shift) % count) for i in range(count)]


def on_device(query, keys, values, grad_out, random_owner, random_within, global_ids):
    nz = lax.axis_size("z")
    nh = lax.axis_size("head")
    zi = lax.axis_index("z")
    xi = lax.axis_index("x")
    hi = lax.axis_index("head")
    count = nz * NX
    ctx_index = zi * NX + xi
    tokens, width = query.shape
    features = width // nh
    heads = features // HEAD_DIM
    rows = nh
    unit = (2, BLOCK, features)
    stat = (2 * heads, BLOCK)

    entries = rows * RAND
    owner_all = random_owner.reshape(count, entries)
    within_all = random_within.reshape(count, entries)
    hit = owner_all == ctx_index
    own = jnp.sum(jnp.where(hit, within_all, 0), axis=1).astype(jnp.int32)
    valid = jnp.any(hit, axis=1).astype(jnp.int32)
    owner_mine = lax.dynamic_index_in_dim(owner_all, ctx_index, 0, keepdims=False)
    named = owner_mine[:, None] == jnp.arange(count, dtype=jnp.int32)[None, :]
    entry_row = (jnp.arange(entries, dtype=jnp.int32) // RAND)[:, None]
    row_of = jnp.sum(jnp.where(named, entry_row, 0), axis=0).astype(jnp.int32)
    global_mine = lax.dynamic_slice_in_dim(global_ids, ctx_index * rows, rows, 0)
    row_ids = jnp.arange(rows, dtype=jnp.int32)[:, None]
    slots = jnp.concatenate(
        [row_ids, row_ids + 1, row_ids + 2, global_mine + rows + 2], axis=1
    ).reshape(-1)
    edges = jnp.stack([ctx_index == 0, ctx_index == count - 1]).astype(jnp.int32)

    def split(a, b):
        a = a.reshape(BLOCK, nh, features).transpose(1, 0, 2)
        b = b.reshape(BLOCK, nh, features).transpose(1, 0, 2)
        return jnp.stack([a, b], 1)

    x_rows = lax.all_to_all(split(query, grad_out), "head", split_axis=0, concat_axis=0, tiled=True)
    x_sent = pick_rows(row_of, x_rows, count)
    x_in = lax.all_to_all(x_sent, CTX, split_axis=0, concat_axis=0, tiled=True)

    kv_split = split(keys, values)
    pieces = []
    for s in range(nh):
        piece = lax.dynamic_index_in_dim(kv_split, (hi + s) % nh, 0, keepdims=False)
        pieces.append(piece if s == 0 else lax.ppermute(piece, "head", ring("head", s)))
    places = (hi - jnp.arange(nh, dtype=jnp.int32)) % nh
    kv_rows = put_in_order(places, pieces)
    left = lax.ppermute(kv_rows[rows - 1], CTX, [(i, (i + 1) % count) for i in range(count)])
    right = lax.ppermute(kv_rows[0], CTX, [((i + 1) % count, i) for i in range(count)])
    summary = kv_rows[0]
    for g in range(1, NGLOB):
        came = lax.ppermute(kv_rows[g], CTX, [(0, g)])
        summary = jnp.where(xi == g, came, summary)
    step = nz // 2
    while step:
        pairs = [(z, z + step) for z in range(0, nz, 2 * step)]
        came = lax.ppermute(summary, "z", pairs)
        summary = jnp.where(zi % (2 * step) == step, came, summary)
        step //= 2
    summaries = [summary] + [lax.ppermute(summary, "x", ring("x", s)) for s in range(1, NX)]
    sum_places = (xi - jnp.arange(NX, dtype=jnp.int32)) % NX
    kv_all = extend(sum_places, kv_rows, left, right, summaries)

    row_spec = pl.BlockSpec((1,) + unit, lambda i, *_: (i, 0, 0, 0))
    stat_spec = pl.BlockSpec((1,) + stat, lambda i, *_: (i, 0, 0))
    placed_spec = pl.BlockSpec((1,) + stat, lambda i, *_: (place_of(i, nz), 0, 0))
    half_spec = pl.BlockSpec((1, BLOCK, features), lambda i, *_: (i, 0, 0))
    shape = jax.ShapeDtypeStruct

    stats_loc = call(
        partial(local_stats_body, rows, heads),
        (rows,),
        (slots, edges),
        (x_rows, kv_all),
        [row_spec, whole(kv_all.shape)],
        shape((rows,) + stat, F32),
        stat_spec,
    )
    stats_out = call(
        partial(entry_stats_body, heads),
        (count,),
        (own, valid),
        (x_in, kv_all),
        [row_spec, whole(kv_all.shape)],
        shape((count,) + stat, F32),
        placed_spec,
    )
    stats_in = exchange_small(stats_out)
    ld, ld_out = call(
        partial(combine_body, rows, heads, count, nz),
        (1,),
        (owner_mine, row_of),
        (stats_loc, stats_in),
        [whole(stats_loc.shape), whole(stats_in.shape)],
        (shape((rows,) + stat, F32), shape((count,) + stat, F32)),
        (whole((rows,) + stat), whole((count,) + stat)),
    )
    ld_in = exchange_small(ld_out)
    dq_out, rand_acc = call(
        partial(entry_grads_body, heads),
        (count,),
        (own, valid),
        (x_in, ld_in, kv_all),
        [row_spec, placed_spec, whole(kv_all.shape)],
        (shape((count, BLOCK, features), BF16), shape((rows,) + unit, F32)),
        (half_spec, whole((rows,) + unit)),
    )
    dq_in = lax.all_to_all(dq_out, CTX, split_axis=0, concat_axis=0, tiled=True)

    side_count = 2 + NGLOB
    dq_loc, loc_acc, side = call(
        partial(local_grads_body, rows, heads),
        (rows,),
        (slots, edges),
        (x_rows, ld, kv_all),
        [row_spec, stat_spec, whole(kv_all.shape)],
        (
            shape((rows, BLOCK, features), F32),
            shape((rows,) + unit, F32),
            shape((side_count,) + unit, BF16),
        ),
        (half_spec, whole((rows,) + unit), whole((side_count,) + unit)),
        [pltpu.VMEM(kv_all.shape, F32)],
    )
    from_left = lax.ppermute(side[1], CTX, [(i, (i + 1) % count) for i in range(count)])
    from_right = lax.ppermute(side[0], CTX, [((i + 1) % count, i) for i in range(count)])
    summed = lax.dynamic_index_in_dim(side, 2 + xi, 0, keepdims=False).astype(F32)
    for s in range(1, NX):
        sent = lax.dynamic_index_in_dim(side, 2 + (xi + s) % NX, 0, keepdims=False)
        summed = summed + lax.ppermute(sent, "x", ring("x", s)).astype(F32)
    step = 1
    while step < nz:
        pairs = [(z + step, z) for z in range(0, nz, 2 * step)]
        summed = summed + lax.ppermute(summed, "z", pairs)
        step *= 2
    total = summed.astype(BF16)
    totals = [total] + [lax.ppermute(total, CTX, [(g, 0)]) for g in range(1, NGLOB)]

    kv_back = call(
        partial(finish_kv_body, rows),
        (rows,),
        (edges,),
        (loc_acc, rand_acc, from_left, from_right, *totals),
        [row_spec, row_spec] + [whole(unit)] * (2 + NGLOB),
        shape((rows,) + unit, BF16),
        row_spec,
    )
    kv_done = lax.all_to_all(kv_back, "head", split_axis=0, concat_axis=0, tiled=True)

    def random_spec(j):
        return pl.BlockSpec((1, BLOCK, features), lambda i, t: (t[i * RAND + j], 0, 0))

    q_back = call(
        finish_q_body,
        (rows,),
        (owner_mine,),
        (dq_loc, dq_in, dq_in, dq_in),
        [half_spec] + [random_spec(j) for j in range(RAND)],
        shape((rows, BLOCK, features), BF16),
        half_spec,
    )
    q_done = lax.all_to_all(q_back, "head", split_axis=0, concat_axis=0, tiled=True)

    def joined(a):
        return a.transpose(1, 0, 2).reshape(tokens, width)

    return joined(q_done), joined(kv_done[:, 0]), joined(kv_done[:, 1])


def solution(mesh):
    count, nh = mesh.devices.shape
    fine = Mesh(mesh.devices.reshape(count // NX, NX, nh), ("z", "x", "head"))
    tokens = P(("z", "x", "head"), None)
    return jax.shard_map(
        on_device,
        mesh=fine,
        in_specs=(tokens,) * 4 + (P(),) * 3,
        out_specs=(tokens,) * 3,
        check_vma=False,
    )
```

```python
from functools import partial

import jax
import jax.numpy as jnp
from jax import lax
from jax.experimental import pallas as pl
from jax.experimental.pallas import tpu as pltpu
from jax.sharding import Mesh, PartitionSpec as P

HEAD_DIM = 128
BLOCK = 128
RAND = 3
GLOB = 2
NGLOB = 4
NX = 4
SLOTS = 3 + GLOB
BF16 = jnp.bfloat16
F32 = jnp.float32
VMEM_LIMIT = 58 * 1024 * 1024
SCALE = HEAD_DIM ** (-0.5)
CTX = ("z", "x")
PER_STEP = 4
GROUP = 8
PARTS = 4
FAR = 1e30


def dot_nt(a, b):
    return lax.dot_general(a, b, (((1,), (1,)), ((), ())), preferred_element_type=F32)


def dot_nn(a, b):
    return lax.dot_general(a, b, (((1,), (0,)), ((), ())), preferred_element_type=F32)


def dot_tn(a, b):
    return lax.dot_general(a, b, (((0,), (0,)), ((), ())), preferred_element_type=F32)


def params():
    return pltpu.CompilerParams(vmem_limit_bytes=VMEM_LIMIT)


def whole(shape):
    return pl.BlockSpec(shape, lambda *_: (0,) * len(shape))


def call(body, grid, scalars, ins, in_specs, out_shape, out_specs, scratch=()):
    return pl.pallas_call(
        body,
        grid_spec=pltpu.PrefetchScalarGridSpec(
            num_scalar_prefetch=len(scalars),
            grid=grid,
            in_specs=in_specs,
            out_specs=out_specs,
            scratch_shapes=list(scratch),
        ),
        out_shape=out_shape,
        compiler_params=params(),
    )(*scalars, *ins)


def pick_body(count, row_ref, x_ref, o_ref, sems):
    copies = [
        pltpu.make_async_copy(x_ref.at[row_ref[i]], o_ref.at[i], sems.at[i]) for i in range(count)
    ]
    for copy in copies:
        copy.start()
    for copy in copies:
        copy.wait()


def pick_rows(rows_of, x, count):
    return call(
        partial(pick_body, count),
        (1,),
        (rows_of,),
        (x,),
        [whole(x.shape)],
        jax.ShapeDtypeStruct((count,) + x.shape[1:], x.dtype),
        pl.BlockSpec(memory_space=pl.ANY),
        [pltpu.SemaphoreType.DMA((count,))],
    )


def cut_body(count, place_ref, a_ref, b_ref, *outs):
    features = a_ref.shape[1] // count
    for s in range(count):
        start = pl.multiple_of(place_ref[s] * features, features)
        outs[s][0] = a_ref[:, pl.ds(start, features)]
        outs[s][1] = b_ref[:, pl.ds(start, features)]


def cut(places, a, b, count):
    unit = (2, a.shape[0], a.shape[1] // count)
    return call(
        partial(cut_body, count),
        (1,),
        (places,),
        (a, b),
        [whole(a.shape)] * 2,
        [jax.ShapeDtypeStruct(unit, a.dtype)] * count,
        [whole(unit)] * count,
    )


def joined_body(count, place_ref, *refs):
    a_ref, b_ref = refs[count:]
    features = a_ref.shape[1] // count
    for s in range(count):
        start = pl.multiple_of(place_ref[s] * features, features)
        a_ref[:, pl.ds(start, features)] = refs[s][0]
        b_ref[:, pl.ds(start, features)] = refs[s][1]


def joined(places, pieces):
    count = len(pieces)
    _, tokens, features = pieces[0].shape
    shape = (tokens, features * count)
    return call(
        partial(joined_body, count),
        (1,),
        (places,),
        pieces,
        [whole(pieces[0].shape)] * count,
        [jax.ShapeDtypeStruct(shape, pieces[0].dtype)] * 2,
        [whole(shape)] * 2,
    )


def order_body(count, place_ref, *refs):
    out = refs[count]
    for s in range(count):
        out[place_ref[s]] = refs[s][...]


def put_in_order(places, pieces):
    count = len(pieces)
    shape = pieces[0].shape
    return call(
        partial(order_body, count),
        (1,),
        (places,),
        pieces,
        [whole(shape)] * count,
        jax.ShapeDtypeStruct((count,) + shape, pieces[0].dtype),
        whole((count,) + shape),
    )


def extend_body(rows, kv_ref, left_ref, right_ref, out):
    out[0] = left_ref[...]
    for r in range(rows):
        out[1 + r] = kv_ref[r]
    out[rows + 1] = right_ref[...]


def extend(kv_rows, left, right):
    rows = kv_rows.shape[0]
    shape = left.shape
    full = (rows + 2,) + shape
    return call(
        partial(extend_body, rows),
        (1,),
        (),
        (kv_rows, left, right),
        [whole(kv_rows.shape)] + [whole(shape)] * 2,
        jax.ShapeDtypeStruct(full, kv_rows.dtype),
        whole(full),
    )


def columns(h):
    return slice(h * HEAD_DIM, (h + 1) * HEAD_DIM)


def row_stats(tiles):
    s = [masked(dot_nt(t[0], t[2]) * SCALE, t[4]) for t in tiles]
    dp = [dot_nt(t[1], t[3]) for t in tiles]
    top = [jnp.max(a, axis=0, keepdims=True) for a in s]
    p = [jnp.exp(a - m) for a, m in zip(s, top)]
    total = [jnp.sum(a, axis=0, keepdims=True) for a in p]
    mean = [jnp.sum(a * b, axis=0, keepdims=True) / n for a, b, n in zip(p, dp, total)]
    return [(m + jnp.log(n), x) for m, n, x in zip(top, total, mean)]


def groups(items, size):
    return [items[i : i + size] for i in range(0, len(items), size)]


def masked(s, masks):
    if masks is None:
        return s
    parts = [s[j * BLOCK : (j + 1) * BLOCK] for j in range(len(masks))]
    parts = [x if m is None else jnp.where(m, -jnp.inf, x) for x, m in zip(parts, masks)]
    return jnp.concatenate(parts, 0) if len(parts) > 1 else parts[0]


def stacked(kv_ref, slots, t, cols):
    return jnp.concatenate([kv_ref[j, t, :, cols] for j in slots], 0)


def band_stats_body(rows, heads, edge_ref, x_ref, kv_ref, o_ref):
    row = pl.program_id(0)
    off_left = (row == 0) & (edge_ref[0] != 0)
    off_right = (row == rows - 1) & (edge_ref[1] != 0)
    slots = [row, row + 1, row + 2]
    for some in groups(range(heads), 2):
        tiles = [
            (
                stacked(kv_ref, slots, 0, columns(h)),
                stacked(kv_ref, slots, 1, columns(h)),
                x_ref[0, 0, :, columns(h)],
                x_ref[0, 1, :, columns(h)],
                [off_left, None, off_right],
            )
            for h in some
        ]
        for h, (log, mean) in zip(some, row_stats(tiles)):
            o_ref[0, h : h + 1, :] = log
            o_ref[0, heads + h : heads + h + 1, :] = mean


def summary_stats_body(rows, heads, slot_ref, x_ref, kv_ref, o_ref):
    row = pl.program_id(0)
    slots = [slot_ref[row * GLOB + j] for j in range(GLOB)]
    for some in groups(range(heads), 4):
        tiles = [
            (
                stacked(kv_ref, slots, 0, columns(h)),
                stacked(kv_ref, slots, 1, columns(h)),
                x_ref[0, 0, :, columns(h)],
                x_ref[0, 1, :, columns(h)],
                None,
            )
            for h in some
        ]
        for h, (log, mean) in zip(some, row_stats(tiles)):
            o_ref[0, h : h + 1, :] = log
            o_ref[0, heads + h : heads + h + 1, :] = mean


def place_of(e, nz):
    return (e % NX) * nz + e // NX


def entry_tiles(heads):
    return groups([(i, h) for i in range(PER_STEP) for h in range(heads)], GROUP)


def entry_stats_body(heads, nz, own_ref, x_ref, kv_ref, o_ref):
    base = pl.program_id(0) * PER_STEP
    for some in entry_tiles(heads):
        tiles = [
            (
                kv_ref[own_ref[base + i], 0, :, columns(h)],
                kv_ref[own_ref[base + i], 1, :, columns(h)],
                x_ref[i, 0, :, columns(h)],
                x_ref[i, 1, :, columns(h)],
                None,
            )
            for i, h in some
        ]
        for (i, h), (log, mean) in zip(some, row_stats(tiles)):
            place = place_of(base + i, nz)
            o_ref[place, h : h + 1, :] = log
            o_ref[place, heads + h : heads + h + 1, :] = mean


def combine_body(
    rows, heads, count, nz, owner_ref, row_ref, band_ref, sum_ref, rem_ref, ld_ref, out_ref
):
    for r in range(rows):
        parts = [band_ref[r], sum_ref[r]]
        for j in range(RAND):
            o = owner_ref[r * RAND + j]
            parts.append(rem_ref[place_of(o, nz)])
        logs = [p[:heads] for p in parts]
        means = [p[heads:] for p in parts]
        top = logs[0]
        for x in logs[1:]:
            top = jnp.maximum(top, x)
        weights = [jnp.exp(x - top) for x in logs]
        total = sum(weights[1:], weights[0])
        mean = sum([w * m for w, m in zip(weights[1:], means[1:])], weights[0] * means[0])
        ld_ref[r, :heads] = top + jnp.log(total)
        ld_ref[r, heads:] = mean / total
    for o in range(count):
        out_ref[place_of(o, nz)] = ld_ref[row_ref[o]]


def pairs(tiles):
    s = [masked(dot_nt(t[0], t[2]) * SCALE, t[6]) for t in tiles]
    dp = [dot_nt(t[1], t[3]) for t in tiles]
    p = [jnp.exp(a - t[4]) for a, t in zip(s, tiles)]
    ds = [(a * (b - t[5])).astype(BF16) for a, b, t in zip(p, dp, tiles)]
    return [a.astype(BF16) for a in p], ds


def grads(tiles):
    p, ds = pairs(tiles)
    dk = [dot_nn(a, t[2]) for a, t in zip(ds, tiles)]
    dv = [dot_nn(a, t[3]) for a, t in zip(p, tiles)]
    dq = [dot_tn(a, t[0]) for a, t in zip(ds, tiles)]
    return zip(dk, dv, dq)


def entry_queries_body(heads, nz, part, own_ref, valid_ref, x_ref, ld_ref, kv_ref, *refs):
    dq_ref, pair_ref = refs[-2:]
    base = (part * pl.num_programs(0) + pl.program_id(0)) * PER_STEP
    far = [jnp.where(valid_ref[base + i] != 0, 0.0, FAR) for i in range(PER_STEP)]
    place = [place_of(base + i, nz) for i in range(PER_STEP)]
    for some in entry_tiles(heads):
        tiles = [
            (
                kv_ref[own_ref[base + i], 0, :, columns(h)],
                kv_ref[own_ref[base + i], 1, :, columns(h)],
                x_ref[i, 0, :, columns(h)],
                x_ref[i, 1, :, columns(h)],
                ld_ref[place[i], h : h + 1, :] + far[i],
                ld_ref[place[i], heads + h : heads + h + 1, :],
                None,
            )
            for i, h in some
        ]
        p, ds = pairs(tiles)
        for (i, h), a, b in zip(some, p, ds):
            pair_ref[i, 0, h] = b
            pair_ref[i, 1, h] = a
        dq = [dot_tn(a, t[0]) for a, t in zip(ds, tiles)]
        for (i, h), a in zip(some, dq):
            dq_ref[i, :, columns(h)] = (a * SCALE).astype(BF16)


def entry_keys_body(heads, own_ref, x_ref, pair_ref, acc_ref):
    step = pl.program_id(0)

    @pl.when(step == 0)
    def _():
        acc_ref[...] = jnp.zeros_like(acc_ref)

    for i in range(PER_STEP):
        own = own_ref[step * PER_STEP + i]
        tiles = [(t, h) for t in range(2) for h in range(heads)]
        terms = [dot_nn(pair_ref[i, t, h], x_ref[i, t, :, columns(h)]) for t, h in tiles]
        for (t, h), term in zip(tiles, terms):
            acc_ref[own, t, :, columns(h)] += term


def row_tile(x_ref, ld_ref, heads, h, keys, vals, masks):
    return (
        keys,
        vals,
        x_ref[0, 0, :, columns(h)],
        x_ref[0, 1, :, columns(h)],
        ld_ref[0, h : h + 1, :],
        ld_ref[0, heads + h : heads + h + 1, :],
        masks,
    )


def early_grads_body(
    rows, heads, slot_ref, edge_ref, x_ref, ld_ref, sum_ref, left_ref, right_ref, *refs
):
    dq_ref, side_ref, acc_ref = refs
    row = pl.program_id(0)

    @pl.when(row == 0)
    def _():
        acc_ref[...] = jnp.zeros_like(acc_ref)

    slots = [slot_ref[row * GLOB + j] for j in range(GLOB)]
    tile = partial(row_tile, x_ref, ld_ref, heads)
    for some in groups(range(heads), 4):
        tiles = [
            tile(h, stacked(sum_ref, slots, 0, columns(h)), stacked(sum_ref, slots, 1, columns(h)), None)
            for h in some
        ]
        for h, (dk, dv, dq) in zip(some, grads(tiles)):
            dq_ref[0, :, columns(h)] = dq
            for n, j in enumerate(slots):
                acc_ref[j, 0, :, columns(h)] += dk[n * BLOCK : (n + 1) * BLOCK]
                acc_ref[j, 1, :, columns(h)] += dv[n * BLOCK : (n + 1) * BLOCK]

    def at_edge(source_ref, off, place):
        for some in groups(range(heads), 4):
            tiles = [
                tile(h, source_ref[0, :, columns(h)], source_ref[1, :, columns(h)], [off])
                for h in some
            ]
            for h, (dk, dv, dq) in zip(some, grads(tiles)):
                dq_ref[0, :, columns(h)] += dq
                side_ref[place, 0, :, columns(h)] = (dk * SCALE).astype(BF16)
                side_ref[place, 1, :, columns(h)] = dv.astype(BF16)

    @pl.when(row == 0)
    def _():
        at_edge(left_ref, edge_ref[0] != 0, 0)

    @pl.when(row == rows - 1)
    def _():
        at_edge(right_ref, edge_ref[1] != 0, 1)
        for n in range(NGLOB):
            side_ref[2 + n, 0] = (acc_ref[n, 0] * SCALE).astype(BF16)
            side_ref[2 + n, 1] = acc_ref[n, 1].astype(BF16)


def late_grads_body(rows, heads, x_ref, ld_ref, kv_ref, begun_ref, dq_ref, acc_ref):
    row = pl.program_id(0)

    @pl.when(row == 0)
    def _():
        acc_ref[...] = jnp.zeros_like(acc_ref)

    slots = [row, row + 1, row + 2]
    masks = [row == 0, None, row == rows - 1]
    tile = partial(row_tile, x_ref, ld_ref, heads)
    for some in groups(range(heads), 2):
        tiles = [
            tile(h, stacked(kv_ref, slots, 0, columns(h)), stacked(kv_ref, slots, 1, columns(h)), masks)
            for h in some
        ]
        for h, (dk, dv, dq) in zip(some, grads(tiles)):
            dq_ref[0, :, columns(h)] = (dq + begun_ref[0, :, columns(h)]) * SCALE
            for n, j in enumerate(slots):
                acc_ref[j, 0, :, columns(h)] += dk[n * BLOCK : (n + 1) * BLOCK]
                acc_ref[j, 1, :, columns(h)] += dv[n * BLOCK : (n + 1) * BLOCK]


def finish_kv_body(rows, place_ref, first_ref, loc_ref, *refs):
    rand_ref, left_ref, right_ref = refs[:3]
    sums = refs[3 : 3 + NGLOB]
    outs = refs[3 + NGLOB :]
    for s in range(rows):
        row = place_ref[s]
        at_first = (row == 0).astype(F32)
        at_last = (row == rows - 1).astype(F32)
        for t in range(2):
            total = loc_ref[row + 1, t] + rand_ref[row, t]
            if t == 0:
                total = total * SCALE
            outs[s][t] = (
                total + at_first * left_ref[t].astype(F32) + at_last * right_ref[t].astype(F32)
            ).astype(BF16)
        for n, sum_ref in enumerate(sums):

            @pl.when((row == n) & (first_ref[0] != 0))
            def _(n=n, s=s, row=row, sum_ref=sum_ref, at_first=at_first, at_last=at_last):
                for t in range(2):
                    total = loc_ref[row + 1, t] + rand_ref[row, t]
                    if t == 0:
                        total = total * SCALE
                    total += at_first * left_ref[t].astype(F32)
                    total += at_last * right_ref[t].astype(F32)
                    outs[s][t] = (total + sum_ref[t].astype(F32)).astype(BF16)


def finish_q_body(rows, owner_ref, loc_ref, in_ref, o_ref):
    for r in range(rows):
        total = loc_ref[r]
        for j in range(RAND):
            total += in_ref[owner_ref[r * RAND + j]].astype(F32)
        o_ref[r] = total.astype(BF16)


def exchange_small(x):
    nz = lax.axis_size("z")
    x = x.reshape((NX, nz) + x.shape[1:])
    x = lax.all_to_all(x, "x", split_axis=0, concat_axis=0, tiled=True)
    x = lax.all_to_all(x, "z", split_axis=1, concat_axis=1, tiled=True)
    return x.reshape((NX * nz,) + x.shape[2:])


def ring(axis, shift):
    count = lax.axis_size(axis)
    return [(i, (i + shift) % count) for i in range(count)]


def on_device(query, keys, values, grad_out, random_owner, random_within, global_ids):
    nz = lax.axis_size("z")
    nh = lax.axis_size("head")
    zi = lax.axis_index("z")
    xi = lax.axis_index("x")
    hi = lax.axis_index("head")
    count = nz * NX
    ctx_index = zi * NX + xi
    tokens, width = query.shape
    features = width // nh
    heads = features // HEAD_DIM
    rows = nh
    unit = (2, BLOCK, features)
    stat = (2 * heads, BLOCK)
    shape = jax.ShapeDtypeStruct

    entries = rows * RAND
    owner_all = random_owner.reshape(count, entries)
    within_all = random_within.reshape(count, entries)
    hit = owner_all == ctx_index
    own = jnp.sum(jnp.where(hit, within_all, 0), axis=1).astype(jnp.int32)
    valid = jnp.any(hit, axis=1).astype(jnp.int32)
    owner_mine = lax.dynamic_index_in_dim(owner_all, ctx_index, 0, keepdims=False)
    named = owner_mine[:, None] == jnp.arange(count, dtype=jnp.int32)[None, :]
    entry_row = (jnp.arange(entries, dtype=jnp.int32) // RAND)[:, None]
    row_of = jnp.sum(jnp.where(named, entry_row, 0), axis=0).astype(jnp.int32)
    global_mine = lax.dynamic_slice_in_dim(global_ids, ctx_index * rows, rows, 0)
    slots = global_mine.reshape(-1)
    edges = jnp.stack([ctx_index == 0, ctx_index == count - 1]).astype(jnp.int32)
    heads_ids = jnp.arange(nh, dtype=jnp.int32)
    sent_to = (hi + heads_ids) % nh
    came_from = (hi - heads_ids) % nh

    x_split = jnp.stack(
        [
            query.reshape(BLOCK, nh, features).transpose(1, 0, 2),
            grad_out.reshape(BLOCK, nh, features).transpose(1, 0, 2),
        ],
        1,
    )
    x_rows = lax.all_to_all(x_split, "head", split_axis=0, concat_axis=0, tiled=True)

    x_sent = pick_rows(row_of, x_rows, count)
    x_sent, keys, values = lax.optimization_barrier((x_sent, keys, values))
    x_in = lax.all_to_all(x_sent, CTX, split_axis=0, concat_axis=0, tiled=True)

    kv_cut = cut(sent_to, keys, values, nh)
    pieces = [kv_cut[0]] + [lax.ppermute(kv_cut[s], "head", ring("head", s)) for s in range(1, nh)]
    kv_rows = put_in_order(came_from, pieces)
    left = lax.ppermute(kv_rows[rows - 1], CTX, [(i, (i + 1) % count) for i in range(count)])
    right = lax.ppermute(kv_rows[0], CTX, [((i + 1) % count, i) for i in range(count)])

    summary = kv_rows[0]
    for g in range(1, NGLOB):
        came = lax.ppermute(kv_rows[g], CTX, [(0, g)])
        summary = jnp.where(xi == g, came, summary)
    step = nz // 2
    while step:
        pairs = [(z, z + step) for z in range(0, nz, 2 * step)]
        came = lax.ppermute(summary, "z", pairs)
        summary = jnp.where(zi % (2 * step) == step, came, summary)
        step //= 2
    row_spec = pl.BlockSpec((1,) + unit, lambda i, *_: (i, 0, 0, 0))
    step_spec = pl.BlockSpec((PER_STEP,) + unit, lambda i, *_: (i, 0, 0, 0))
    stat_spec = pl.BlockSpec((1,) + stat, lambda i, *_: (i, 0, 0))
    half_spec = pl.BlockSpec((1, BLOCK, features), lambda i, *_: (i, 0, 0))

    stats_out = call(
        partial(entry_stats_body, heads, nz),
        (count // PER_STEP,),
        (own,),
        (x_in, kv_rows),
        [step_spec, whole(kv_rows.shape)],
        shape((count,) + stat, F32),
        whole((count,) + stat),
    )
    stats_out, left, right, summary = lax.optimization_barrier((stats_out, left, right, summary))
    kv_band = extend(kv_rows, left, right)
    summaries = [summary] + [lax.ppermute(summary, "x", ring("x", s)) for s in range(1, NX)]
    sum_places = (xi - jnp.arange(NX, dtype=jnp.int32)) % NX
    kv_sum = put_in_order(sum_places, summaries)
    stats_band = call(
        partial(band_stats_body, rows, heads),
        (rows,),
        (edges,),
        (x_rows, kv_band),
        [row_spec, whole(kv_band.shape)],
        shape((rows,) + stat, F32),
        stat_spec,
    )
    stats_sum = call(
        partial(summary_stats_body, rows, heads),
        (rows,),
        (slots,),
        (x_rows, kv_sum),
        [row_spec, whole(kv_sum.shape)],
        shape((rows,) + stat, F32),
        stat_spec,
    )
    stats_in = exchange_small(stats_out)
    ld, ld_out = call(
        partial(combine_body, rows, heads, count, nz),
        (1,),
        (owner_mine, row_of),
        (stats_band, stats_sum, stats_in),
        [whole(stats_band.shape)] * 2 + [whole(stats_in.shape)],
        (shape((rows,) + stat, F32), shape((count,) + stat, F32)),
        (whole((rows,) + stat), whole((count,) + stat)),
    )
    ld_in = exchange_small(ld_out)

    side_count = 2 + NGLOB
    dq_early, side = call(
        partial(early_grads_body, rows, heads),
        (rows,),
        (slots, edges),
        (x_rows, ld, kv_sum, left, right),
        [row_spec, stat_spec, whole(kv_sum.shape), whole(unit), whole(unit)],
        (shape((rows, BLOCK, features), F32), shape((side_count,) + unit, BF16)),
        (half_spec, whole((side_count,) + unit)),
        [pltpu.VMEM((NGLOB,) + unit, F32)],
    )
    ld_in, side = lax.optimization_barrier((ld_in, side))
    from_left = lax.ppermute(side[1], CTX, [(i, (i + 1) % count) for i in range(count)])
    from_right = lax.ppermute(side[0], CTX, [((i + 1) % count, i) for i in range(count)])
    summed = lax.dynamic_index_in_dim(side, 2 + xi, 0, keepdims=False).astype(F32)
    for s in range(1, NX):
        sent = lax.dynamic_index_in_dim(side, 2 + (xi + s) % NX, 0, keepdims=False)
        summed = summed + lax.ppermute(sent, "x", ring("x", s)).astype(F32)
    part_steps = count // PER_STEP // PARTS
    dq_out = pairs_out = None
    hop = 1
    for part in range(PARTS):

        def at_part(i, *_, part=part):
            return (part * part_steps + i, 0, 0, 0)

        def half_part(i, *_, part=part):
            return (part * part_steps + i, 0, 0)

        def pair_part(i, *_, part=part):
            return (part * part_steps + i, 0, 0, 0, 0)

        pair_shape = (2, heads, BLOCK, BLOCK)
        dq_out, pairs_out = pl.pallas_call(
            partial(entry_queries_body, heads, nz, part),
            grid_spec=pltpu.PrefetchScalarGridSpec(
                num_scalar_prefetch=2,
                grid=(part_steps,),
                in_specs=[
                    pl.BlockSpec((PER_STEP,) + unit, at_part),
                    whole((count,) + stat),
                    whole(kv_rows.shape),
                ]
                + ([pl.BlockSpec(memory_space=pl.ANY)] * 2 if part else []),
                out_specs=(
                    pl.BlockSpec((PER_STEP, BLOCK, features), half_part),
                    pl.BlockSpec((PER_STEP,) + pair_shape, pair_part),
                ),
            ),
            out_shape=(
                shape((count, BLOCK, features), BF16),
                shape((count,) + pair_shape, BF16),
            ),
            input_output_aliases={5: 0, 6: 1} if part else {},
            compiler_params=params(),
        )(own, valid, x_in, ld_in, kv_rows, *([dq_out, pairs_out] if part else []))
        dq_out, summed = lax.optimization_barrier((dq_out, summed))
        if hop < nz:
            links = [(z + hop, z) for z in range(0, nz, 2 * hop)]
            summed = summed + lax.ppermute(summed.astype(BF16), "z", links).astype(F32)
            hop *= 2
    dq_out, summed, from_left, from_right = lax.optimization_barrier(
        (dq_out, summed, from_left, from_right)
    )
    dq_in = lax.all_to_all(dq_out, CTX, split_axis=0, concat_axis=0, tiled=True)

    rand_acc = call(
        partial(entry_keys_body, heads),
        (count // PER_STEP,),
        (own,),
        (x_in, pairs_out),
        [step_spec, pl.BlockSpec((PER_STEP,) + pair_shape, lambda i, *_: (i, 0, 0, 0, 0))],
        shape((rows,) + unit, F32),
        whole((rows,) + unit),
    )
    total = summed.astype(BF16)
    totals = [total] + [lax.ppermute(total, CTX, [(g, 0)]) for g in range(1, NGLOB)]
    dq_loc, loc_acc = call(
        partial(late_grads_body, rows, heads),
        (rows,),
        (),
        (x_rows, ld, kv_band, dq_early),
        [row_spec, stat_spec, whole(kv_band.shape), half_spec],
        (shape((rows, BLOCK, features), F32), shape((rows + 2,) + unit, F32)),
        (half_spec, whole((rows + 2,) + unit)),
    )
    kv_back = call(
        partial(finish_kv_body, rows),
        (1,),
        (sent_to, edges),
        (loc_acc, rand_acc, from_left, from_right, *totals),
        [whole((rows + 2,) + unit), whole((rows,) + unit)] + [whole(unit)] * (2 + NGLOB),
        [shape(unit, BF16)] * rows,
        [whole(unit)] * rows,
    )
    kv_done = [kv_back[0]]
    for s in range(1, nh):
        kv_done.append(lax.ppermute(kv_back[s], "head", ring("head", s)))
    grad_keys, grad_values = joined(came_from, kv_done)
    dq_in, grad_keys, grad_values = lax.optimization_barrier((dq_in, grad_keys, grad_values))

    q_back = call(
        partial(finish_q_body, rows),
        (1,),
        (owner_mine,),
        (dq_loc, dq_in),
        [whole(dq_loc.shape), whole(dq_in.shape)],
        shape((rows, BLOCK, features), BF16),
        whole((rows, BLOCK, features)),
    )
    q_done = lax.all_to_all(q_back, "head", split_axis=0, concat_axis=0, tiled=True)
    return q_done.transpose(1, 0, 2).reshape(tokens, width), grad_keys, grad_values


def solution(mesh):
    count, nh = mesh.devices.shape
    fine = Mesh(mesh.devices.reshape(count // NX, NX, nh), ("z", "x", "head"))
    tokens = P(("z", "x", "head"), None)
    return jax.shard_map(
        on_device,
        mesh=fine,
        in_specs=(tokens,) * 4 + (P(),) * 3,
        out_specs=(tokens,) * 3,
        check_vma=False,
    )
```

```python
from functools import partial

import jax
import jax.numpy as jnp
from jax import lax
from jax.experimental import pallas as pl
from jax.experimental.pallas import tpu as pltpu
from jax.sharding import Mesh, PartitionSpec as P

HEAD_DIM = 128
BLOCK = 128
RAND = 3
GLOB = 2
NGLOB = 4
NX = 4
SLOTS = 3 + GLOB
BF16 = jnp.bfloat16
F32 = jnp.float32
VMEM_LIMIT = 58 * 1024 * 1024
SCALE = HEAD_DIM ** (-0.5)
CTX = ("z", "x")
PER_STEP = 4
GROUP = 8
PARTS = 4
FAR = 1e30


def dot_nt(a, b):
    return lax.dot_general(a, b, (((1,), (1,)), ((), ())), preferred_element_type=F32)


def dot_nn(a, b):
    return lax.dot_general(a, b, (((1,), (0,)), ((), ())), preferred_element_type=F32)


def dot_tn(a, b):
    return lax.dot_general(a, b, (((0,), (0,)), ((), ())), preferred_element_type=F32)


def params():
    return pltpu.CompilerParams(vmem_limit_bytes=VMEM_LIMIT)


def whole(shape):
    return pl.BlockSpec(shape, lambda *_: (0,) * len(shape))


def call(body, grid, scalars, ins, in_specs, out_shape, out_specs, scratch=()):
    return pl.pallas_call(
        body,
        grid_spec=pltpu.PrefetchScalarGridSpec(
            num_scalar_prefetch=len(scalars),
            grid=grid,
            in_specs=in_specs,
            out_specs=out_specs,
            scratch_shapes=list(scratch),
        ),
        out_shape=out_shape,
        compiler_params=params(),
    )(*scalars, *ins)


def pick_body(count, row_ref, x_ref, o_ref, sems):
    copies = [
        pltpu.make_async_copy(x_ref.at[row_ref[i]], o_ref.at[i], sems.at[i]) for i in range(count)
    ]
    for copy in copies:
        copy.start()
    for copy in copies:
        copy.wait()


def pick_rows(rows_of, x, count):
    return call(
        partial(pick_body, count),
        (1,),
        (rows_of,),
        (x,),
        [whole(x.shape)],
        jax.ShapeDtypeStruct((count,) + x.shape[1:], x.dtype),
        pl.BlockSpec(memory_space=pl.ANY),
        [pltpu.SemaphoreType.DMA((count,))],
    )


def cut_body(count, place_ref, a_ref, b_ref, *outs):
    features = a_ref.shape[1] // count
    for s in range(count):
        start = pl.multiple_of(place_ref[s] * features, features)
        outs[s][0] = a_ref[:, pl.ds(start, features)]
        outs[s][1] = b_ref[:, pl.ds(start, features)]


def cut(places, a, b, count):
    unit = (2, a.shape[0], a.shape[1] // count)
    return call(
        partial(cut_body, count),
        (1,),
        (places,),
        (a, b),
        [whole(a.shape)] * 2,
        [jax.ShapeDtypeStruct(unit, a.dtype)] * count,
        [whole(unit)] * count,
    )


def joined_body(count, parts, place_ref, *refs):
    outs = refs[count:]
    features = outs[0].shape[1] // count
    for s in range(count):
        start = pl.multiple_of(place_ref[s] * features, features)
        for t in range(parts):
            outs[t][:, pl.ds(start, features)] = refs[s][t]


def joined(places, pieces):
    count = len(pieces)
    parts, tokens, features = pieces[0].shape
    shape = (tokens, features * count)
    return call(
        partial(joined_body, count, parts),
        (1,),
        (places,),
        pieces,
        [whole(pieces[0].shape)] * count,
        [jax.ShapeDtypeStruct(shape, pieces[0].dtype)] * parts,
        [whole(shape)] * parts,
    )


def order_body(count, place_ref, *refs):
    out = refs[count]
    for s in range(count):
        out[place_ref[s]] = refs[s][...]


def put_in_order(places, pieces):
    count = len(pieces)
    shape = pieces[0].shape
    return call(
        partial(order_body, count),
        (1,),
        (places,),
        pieces,
        [whole(shape)] * count,
        jax.ShapeDtypeStruct((count,) + shape, pieces[0].dtype),
        whole((count,) + shape),
    )


def columns(h):
    return slice(h * HEAD_DIM, (h + 1) * HEAD_DIM)


def row_stats(tiles):
    s = [masked(dot_nt(t[0], t[2]) * SCALE, t[4]) for t in tiles]
    dp = [dot_nt(t[1], t[3]) for t in tiles]
    top = [jnp.max(a, axis=0, keepdims=True) for a in s]
    p = [jnp.exp(a - m) for a, m in zip(s, top)]
    total = [jnp.sum(a, axis=0, keepdims=True) for a in p]
    mean = [jnp.sum(a * b, axis=0, keepdims=True) / n for a, b, n in zip(p, dp, total)]
    return [(m + jnp.log(n), x) for m, n, x in zip(top, total, mean)]


def groups(items, size):
    return [items[i : i + size] for i in range(0, len(items), size)]


def masked(s, masks):
    if masks is None:
        return s
    parts = [s[j * BLOCK : (j + 1) * BLOCK] for j in range(len(masks))]
    parts = [x if m is None else jnp.where(m, -jnp.inf, x) for x, m in zip(parts, masks)]
    return jnp.concatenate(parts, 0) if len(parts) > 1 else parts[0]


def stacked(kv_ref, slots, t, cols):
    return jnp.concatenate([kv_ref[j, t, :, cols] for j in slots], 0)


def near(row, rows):
    slots = [jnp.maximum(row - 1, 0), row, jnp.minimum(row + 1, rows - 1)]
    return slots, [row == 0, None, row == rows - 1]


def stats_out_of(some, heads, tiles, o_ref):
    for h, (log, mean) in zip(some, row_stats(tiles)):
        o_ref[0, h : h + 1, :] = log
        o_ref[0, heads + h : heads + h + 1, :] = mean


def band_stats_body(rows, heads, x_ref, kv_ref, o_ref):
    slots, masks = near(pl.program_id(0), rows)
    for some in groups(range(heads), 2):
        tiles = [
            (
                stacked(kv_ref, slots, 0, columns(h)),
                stacked(kv_ref, slots, 1, columns(h)),
                x_ref[0, 0, :, columns(h)],
                x_ref[0, 1, :, columns(h)],
                masks,
            )
            for h in some
        ]
        stats_out_of(some, heads, tiles, o_ref)


def far_stats_body(rows, heads, slot_ref, edge_ref, x_ref, kv_ref, left_ref, right_ref, o_ref):
    row = pl.program_id(0)
    slots = [slot_ref[row * GLOB + j] for j in range(GLOB)]

    def tiles_of(some, edge, off):
        def both(t, h):
            parts = [kv_ref[j, t, :, columns(h)] for j in slots]
            return jnp.concatenate(parts + ([] if edge is None else [edge[t, :, columns(h)]]), 0)

        return [
            (
                both(0, h),
                both(1, h),
                x_ref[0, 0, :, columns(h)],
                x_ref[0, 1, :, columns(h)],
                None if edge is None else [None] * GLOB + [off],
            )
            for h in some
        ]

    @pl.when((row > 0) & (row < rows - 1))
    def _():
        for some in groups(range(heads), 4):
            stats_out_of(some, heads, tiles_of(some, None, None), o_ref)

    @pl.when(row == 0)
    def _():
        for some in groups(range(heads), 2):
            stats_out_of(some, heads, tiles_of(some, left_ref, edge_ref[0] != 0), o_ref)

    @pl.when(row == rows - 1)
    def _():
        for some in groups(range(heads), 2):
            stats_out_of(some, heads, tiles_of(some, right_ref, edge_ref[1] != 0), o_ref)


def place_of(e, nz):
    return (e % NX) * nz + e // NX


def entry_tiles(heads):
    return groups([(i, h) for i in range(PER_STEP) for h in range(heads)], GROUP)


def entry_stats_body(heads, nz, own_ref, x_ref, kv_ref, o_ref):
    base = pl.program_id(0) * PER_STEP
    for some in entry_tiles(heads):
        tiles = [
            (
                kv_ref[own_ref[base + i], 0, :, columns(h)],
                kv_ref[own_ref[base + i], 1, :, columns(h)],
                x_ref[i, 0, :, columns(h)],
                x_ref[i, 1, :, columns(h)],
                None,
            )
            for i, h in some
        ]
        for (i, h), (log, mean) in zip(some, row_stats(tiles)):
            place = place_of(base + i, nz)
            o_ref[place, h : h + 1, :] = log
            o_ref[place, heads + h : heads + h + 1, :] = mean


def combine_body(
    rows, heads, count, nz, owner_ref, row_ref, band_ref, sum_ref, rem_ref, ld_ref, out_ref
):
    for r in range(rows):
        parts = [band_ref[r], sum_ref[r]]
        for j in range(RAND):
            o = owner_ref[r * RAND + j]
            parts.append(rem_ref[place_of(o, nz)])
        logs = [p[:heads] for p in parts]
        means = [p[heads:] for p in parts]
        top = logs[0]
        for x in logs[1:]:
            top = jnp.maximum(top, x)
        weights = [jnp.exp(x - top) for x in logs]
        total = sum(weights[1:], weights[0])
        mean = sum([w * m for w, m in zip(weights[1:], means[1:])], weights[0] * means[0])
        ld_ref[r, :heads] = top + jnp.log(total)
        ld_ref[r, heads:] = mean / total
    for o in range(count):
        out_ref[place_of(o, nz)] = ld_ref[row_ref[o]]


def pairs(tiles):
    s = [masked(dot_nt(t[0], t[2]) * SCALE, t[6]) for t in tiles]
    dp = [dot_nt(t[1], t[3]) for t in tiles]
    p = [jnp.exp(a - t[4]) for a, t in zip(s, tiles)]
    ds = [(a * (b - t[5])).astype(BF16) for a, b, t in zip(p, dp, tiles)]
    return [a.astype(BF16) for a in p], ds


def grads(tiles):
    p, ds = pairs(tiles)
    dk = [dot_nn(a, t[2]) for a, t in zip(ds, tiles)]
    dv = [dot_nn(a, t[3]) for a, t in zip(p, tiles)]
    dq = [dot_tn(a, t[0]) for a, t in zip(ds, tiles)]
    return zip(dk, dv, dq)


def entry_queries_body(heads, nz, part, own_ref, valid_ref, x_ref, ld_ref, kv_ref, *refs):
    dq_ref, pair_ref = refs[-2:]
    base = (part * pl.num_programs(0) + pl.program_id(0)) * PER_STEP
    far = [jnp.where(valid_ref[base + i] != 0, 0.0, FAR) for i in range(PER_STEP)]
    place = [place_of(base + i, nz) for i in range(PER_STEP)]
    for some in entry_tiles(heads):
        tiles = [
            (
                kv_ref[own_ref[base + i], 0, :, columns(h)],
                kv_ref[own_ref[base + i], 1, :, columns(h)],
                x_ref[i, 0, :, columns(h)],
                x_ref[i, 1, :, columns(h)],
                ld_ref[place[i], h : h + 1, :] + far[i],
                ld_ref[place[i], heads + h : heads + h + 1, :],
                None,
            )
            for i, h in some
        ]
        p, ds = pairs(tiles)
        for (i, h), a, b in zip(some, p, ds):
            pair_ref[i, 0, h] = b
            pair_ref[i, 1, h] = a
        dq = [dot_tn(a, t[0]) for a, t in zip(ds, tiles)]
        for (i, h), a in zip(some, dq):
            dq_ref[i, :, columns(h)] = (a * SCALE).astype(BF16)


def entry_keys_body(heads, own_ref, x_ref, pair_ref, acc_ref):
    step = pl.program_id(0)

    @pl.when(step == 0)
    def _():
        acc_ref[...] = jnp.zeros_like(acc_ref)

    for i in range(PER_STEP):
        own = own_ref[step * PER_STEP + i]
        tiles = [(t, h) for t in range(2) for h in range(heads)]
        terms = [dot_nn(pair_ref[i, t, h], x_ref[i, t, :, columns(h)]) for t, h in tiles]
        for (t, h), term in zip(tiles, terms):
            acc_ref[own, t, :, columns(h)] += term


def row_tile(x_ref, ld_ref, heads, h, keys, vals, masks):
    return (
        keys,
        vals,
        x_ref[0, 0, :, columns(h)],
        x_ref[0, 1, :, columns(h)],
        ld_ref[0, h : h + 1, :],
        ld_ref[0, heads + h : heads + h + 1, :],
        masks,
    )


def early_grads_body(
    rows, heads, slot_ref, edge_ref, x_ref, ld_ref, sum_ref, left_ref, right_ref, *refs
):
    dq_ref, side_ref, acc_ref = refs
    row = pl.program_id(0)

    @pl.when(row == 0)
    def _():
        acc_ref[...] = jnp.zeros_like(acc_ref)

    slots = [slot_ref[row * GLOB + j] for j in range(GLOB)]
    tile = partial(row_tile, x_ref, ld_ref, heads)
    for some in groups(range(heads), 4):
        tiles = [
            tile(h, stacked(sum_ref, slots, 0, columns(h)), stacked(sum_ref, slots, 1, columns(h)), None)
            for h in some
        ]
        for h, (dk, dv, dq) in zip(some, grads(tiles)):
            dq_ref[0, :, columns(h)] = dq
            for n, j in enumerate(slots):
                acc_ref[j, 0, :, columns(h)] += dk[n * BLOCK : (n + 1) * BLOCK]
                acc_ref[j, 1, :, columns(h)] += dv[n * BLOCK : (n + 1) * BLOCK]

    def at_edge(source_ref, off, place):
        for some in groups(range(heads), 4):
            tiles = [
                tile(h, source_ref[0, :, columns(h)], source_ref[1, :, columns(h)], [off])
                for h in some
            ]
            for h, (dk, dv, dq) in zip(some, grads(tiles)):
                dq_ref[0, :, columns(h)] += dq
                side_ref[place, 0, :, columns(h)] = (dk * SCALE).astype(BF16)
                side_ref[place, 1, :, columns(h)] = dv.astype(BF16)

    @pl.when(row == 0)
    def _():
        at_edge(left_ref, edge_ref[0] != 0, 0)

    @pl.when(row == rows - 1)
    def _():
        at_edge(right_ref, edge_ref[1] != 0, 1)
        for n in range(NGLOB):
            side_ref[2 + n, 0] = (acc_ref[n, 0] * SCALE).astype(BF16)
            side_ref[2 + n, 1] = acc_ref[n, 1].astype(BF16)


def late_grads_body(rows, heads, x_ref, ld_ref, kv_ref, begun_ref, dq_ref, acc_ref):
    row = pl.program_id(0)

    @pl.when(row == 0)
    def _():
        acc_ref[...] = jnp.zeros_like(acc_ref)

    slots, masks = near(row, rows)
    tile = partial(row_tile, x_ref, ld_ref, heads)
    for some in groups(range(heads), 2):
        tiles = [
            tile(h, stacked(kv_ref, slots, 0, columns(h)), stacked(kv_ref, slots, 1, columns(h)), masks)
            for h in some
        ]
        for h, (dk, dv, dq) in zip(some, grads(tiles)):
            dq_ref[0, :, columns(h)] = (dq + begun_ref[0, :, columns(h)]) * SCALE
            for n, j in enumerate(slots):
                acc_ref[j, 0, :, columns(h)] += dk[n * BLOCK : (n + 1) * BLOCK]
                acc_ref[j, 1, :, columns(h)] += dv[n * BLOCK : (n + 1) * BLOCK]


def finish_kv_body(rows, place_ref, first_ref, loc_ref, *refs):
    rand_ref, left_ref, right_ref = refs[:3]
    sums = refs[3 : 3 + NGLOB]
    outs = refs[3 + NGLOB :]
    for s in range(rows):
        row = place_ref[s]
        at_first = (row == 0).astype(F32)
        at_last = (row == rows - 1).astype(F32)
        for t in range(2):
            total = loc_ref[row, t] + rand_ref[row, t]
            if t == 0:
                total = total * SCALE
            outs[s][t] = (
                total + at_first * left_ref[t].astype(F32) + at_last * right_ref[t].astype(F32)
            ).astype(BF16)
        for n, sum_ref in enumerate(sums):

            @pl.when((row == n) & (first_ref[0] != 0))
            def _(n=n, s=s, row=row, sum_ref=sum_ref, at_first=at_first, at_last=at_last):
                for t in range(2):
                    total = loc_ref[row, t] + rand_ref[row, t]
                    if t == 0:
                        total = total * SCALE
                    total += at_first * left_ref[t].astype(F32)
                    total += at_last * right_ref[t].astype(F32)
                    outs[s][t] = (total + sum_ref[t].astype(F32)).astype(BF16)


def finish_q_body(rows, place_ref, owner_ref, loc_ref, in_ref, *outs):
    for s in range(rows):
        row = place_ref[s]
        total = loc_ref[row]
        for j in range(RAND):
            total += in_ref[owner_ref[row * RAND + j]].astype(F32)
        outs[s][0] = total.astype(BF16)


def exchange_small(x):
    nz = lax.axis_size("z")
    x = x.reshape((NX, nz) + x.shape[1:])
    x = lax.all_to_all(x, "x", split_axis=0, concat_axis=0, tiled=True)
    x = lax.all_to_all(x, "z", split_axis=1, concat_axis=1, tiled=True)
    return x.reshape((NX * nz,) + x.shape[2:])


def ring(axis, shift):
    count = lax.axis_size(axis)
    return [(i, (i + shift) % count) for i in range(count)]


def on_device(query, keys, values, grad_out, random_owner, random_within, global_ids):
    nz = lax.axis_size("z")
    nh = lax.axis_size("head")
    zi = lax.axis_index("z")
    xi = lax.axis_index("x")
    hi = lax.axis_index("head")
    count = nz * NX
    ctx_index = zi * NX + xi
    tokens, width = query.shape
    features = width // nh
    heads = features // HEAD_DIM
    rows = nh
    unit = (2, BLOCK, features)
    stat = (2 * heads, BLOCK)
    shape = jax.ShapeDtypeStruct

    entries = rows * RAND
    owner_all = random_owner.reshape(count, entries)
    within_all = random_within.reshape(count, entries)
    hit = owner_all == ctx_index
    own = jnp.sum(jnp.where(hit, within_all, 0), axis=1).astype(jnp.int32)
    valid = jnp.any(hit, axis=1).astype(jnp.int32)
    owner_mine = lax.dynamic_index_in_dim(owner_all, ctx_index, 0, keepdims=False)
    named = owner_mine[:, None] == jnp.arange(count, dtype=jnp.int32)[None, :]
    entry_row = (jnp.arange(entries, dtype=jnp.int32) // RAND)[:, None]
    row_of = jnp.sum(jnp.where(named, entry_row, 0), axis=0).astype(jnp.int32)
    global_mine = lax.dynamic_slice_in_dim(global_ids, ctx_index * rows, rows, 0)
    slots = global_mine.reshape(-1)
    edges = jnp.stack([ctx_index == 0, ctx_index == count - 1]).astype(jnp.int32)
    heads_ids = jnp.arange(nh, dtype=jnp.int32)
    sent_to = (hi + heads_ids) % nh
    came_from = (hi - heads_ids) % nh

    x_split = jnp.stack(
        [
            query.reshape(BLOCK, nh, features).transpose(1, 0, 2),
            grad_out.reshape(BLOCK, nh, features).transpose(1, 0, 2),
        ],
        1,
    )
    x_rows = lax.all_to_all(x_split, "head", split_axis=0, concat_axis=0, tiled=True)

    x_sent = pick_rows(row_of, x_rows, count)
    x_sent, keys, values = lax.optimization_barrier((x_sent, keys, values))
    x_in = lax.all_to_all(x_sent, CTX, split_axis=0, concat_axis=0, tiled=True)

    kv_cut = cut(sent_to, keys, values, nh)
    pieces = [kv_cut[0]] + [lax.ppermute(kv_cut[s], "head", ring("head", s)) for s in range(1, nh)]
    kv_rows = put_in_order(came_from, pieces)
    left = lax.ppermute(kv_rows[rows - 1], CTX, [(i, (i + 1) % count) for i in range(count)])
    right = lax.ppermute(kv_rows[0], CTX, [((i + 1) % count, i) for i in range(count)])

    summary = kv_rows[0]
    for g in range(1, NGLOB):
        came = lax.ppermute(kv_rows[g], CTX, [(0, g)])
        summary = jnp.where(xi == g, came, summary)
    hops = []
    step = nz // 2
    while step:
        hops.append(step)
        step //= 2

    def hop_along(block, step):
        pairs = [(z, z + step) for z in range(0, nz, 2 * step)]
        return lax.ppermute(block, "z", pairs)

    first = hop_along(summary, hops[0])

    row_spec = pl.BlockSpec((1,) + unit, lambda i, *_: (i, 0, 0, 0))
    step_spec = pl.BlockSpec((PER_STEP,) + unit, lambda i, *_: (i, 0, 0, 0))
    stat_spec = pl.BlockSpec((1,) + stat, lambda i, *_: (i, 0, 0))
    half_spec = pl.BlockSpec((1, BLOCK, features), lambda i, *_: (i, 0, 0))

    stats_band = call(
        partial(band_stats_body, rows, heads),
        (rows,),
        (),
        (x_rows, kv_rows),
        [row_spec, whole(kv_rows.shape)],
        shape((rows,) + stat, F32),
        stat_spec,
    )
    stats_band, first = lax.optimization_barrier((stats_band, first))
    x_in, stats_band = lax.optimization_barrier((x_in, stats_band))
    summary = jnp.where(zi % (2 * hops[0]) == hops[0], first, summary)
    second = hop_along(summary, hops[1])
    stats_out = call(
        partial(entry_stats_body, heads, nz),
        (count // PER_STEP,),
        (own,),
        (x_in, kv_rows),
        [step_spec, whole(kv_rows.shape)],
        shape((count,) + stat, F32),
        whole((count,) + stat),
    )
    stats_out, left, right, second = lax.optimization_barrier((stats_out, left, right, second))
    summary = jnp.where(zi % (2 * hops[1]) == hops[1], second, summary)
    for step in hops[2:]:
        summary = jnp.where(zi % (2 * step) == step, hop_along(summary, step), summary)
    summaries = [summary] + [lax.ppermute(summary, "x", ring("x", s)) for s in range(1, NX)]
    sum_places = (xi - jnp.arange(NX, dtype=jnp.int32)) % NX
    kv_sum = put_in_order(sum_places, summaries)
    stats_far = call(
        partial(far_stats_body, rows, heads),
        (rows,),
        (slots, edges),
        (x_rows, kv_sum, left, right),
        [row_spec, whole(kv_sum.shape), whole(unit), whole(unit)],
        shape((rows,) + stat, F32),
        stat_spec,
    )
    stats_in = exchange_small(stats_out)
    ld, ld_out = call(
        partial(combine_body, rows, heads, count, nz),
        (1,),
        (owner_mine, row_of),
        (stats_band, stats_far, stats_in),
        [whole(stats_band.shape)] * 2 + [whole(stats_in.shape)],
        (shape((rows,) + stat, F32), shape((count,) + stat, F32)),
        (whole((rows,) + stat), whole((count,) + stat)),
    )
    ld_in = exchange_small(ld_out)

    side_count = 2 + NGLOB
    dq_early, side = call(
        partial(early_grads_body, rows, heads),
        (rows,),
        (slots, edges),
        (x_rows, ld, kv_sum, left, right),
        [row_spec, stat_spec, whole(kv_sum.shape), whole(unit), whole(unit)],
        (shape((rows, BLOCK, features), F32), shape((side_count,) + unit, BF16)),
        (half_spec, whole((side_count,) + unit)),
        [pltpu.VMEM((NGLOB,) + unit, F32)],
    )
    ld_in, side = lax.optimization_barrier((ld_in, side))
    from_left = lax.ppermute(side[1], CTX, [(i, (i + 1) % count) for i in range(count)])
    from_right = lax.ppermute(side[0], CTX, [((i + 1) % count, i) for i in range(count)])
    summed = lax.dynamic_index_in_dim(side, 2 + xi, 0, keepdims=False).astype(F32)
    for s in range(1, NX):
        sent = lax.dynamic_index_in_dim(side, 2 + (xi + s) % NX, 0, keepdims=False)
        summed = summed + lax.ppermute(sent, "x", ring("x", s)).astype(F32)
    part_steps = count // PER_STEP // PARTS
    dq_out = pairs_out = None
    hop = 1
    for part in range(PARTS):

        def at_part(i, *_, part=part):
            return (part * part_steps + i, 0, 0, 0)

        def half_part(i, *_, part=part):
            return (part * part_steps + i, 0, 0)

        def pair_part(i, *_, part=part):
            return (part * part_steps + i, 0, 0, 0, 0)

        pair_shape = (2, heads, BLOCK, BLOCK)
        dq_out, pairs_out = pl.pallas_call(
            partial(entry_queries_body, heads, nz, part),
            grid_spec=pltpu.PrefetchScalarGridSpec(
                num_scalar_prefetch=2,
                grid=(part_steps,),
                in_specs=[
                    pl.BlockSpec((PER_STEP,) + unit, at_part),
                    whole((count,) + stat),
                    whole(kv_rows.shape),
                ]
                + ([pl.BlockSpec(memory_space=pl.ANY)] * 2 if part else []),
                out_specs=(
                    pl.BlockSpec((PER_STEP, BLOCK, features), half_part),
                    pl.BlockSpec((PER_STEP,) + pair_shape, pair_part),
                ),
            ),
            out_shape=(
                shape((count, BLOCK, features), BF16),
                shape((count,) + pair_shape, BF16),
            ),
            input_output_aliases={5: 0, 6: 1} if part else {},
            compiler_params=params(),
        )(own, valid, x_in, ld_in, kv_rows, *([dq_out, pairs_out] if part else []))
        if part:
            dq_out, summed = lax.optimization_barrier((dq_out, summed))
        else:
            dq_out, summed, from_left, from_right = lax.optimization_barrier(
                (dq_out, summed, from_left, from_right)
            )
        if hop < nz:
            links = [(z + hop, z) for z in range(0, nz, 2 * hop)]
            summed = summed + lax.ppermute(summed.astype(BF16), "z", links).astype(F32)
            hop *= 2
    dq_out, summed = lax.optimization_barrier((dq_out, summed))
    dq_in = lax.all_to_all(dq_out, CTX, split_axis=0, concat_axis=0, tiled=True)

    rand_acc = call(
        partial(entry_keys_body, heads),
        (count // PER_STEP,),
        (own,),
        (x_in, pairs_out),
        [step_spec, pl.BlockSpec((PER_STEP,) + pair_shape, lambda i, *_: (i, 0, 0, 0, 0))],
        shape((rows,) + unit, F32),
        whole((rows,) + unit),
    )
    total = summed.astype(BF16)
    totals = [total] + [lax.ppermute(total, CTX, [(g, 0)]) for g in range(1, NGLOB)]
    dq_loc, loc_acc = call(
        partial(late_grads_body, rows, heads),
        (rows,),
        (),
        (x_rows, ld, kv_rows, dq_early),
        [row_spec, stat_spec, whole(kv_rows.shape), half_spec],
        (shape((rows, BLOCK, features), F32), shape((rows,) + unit, F32)),
        (half_spec, whole((rows,) + unit)),
    )
    kv_back = call(
        partial(finish_kv_body, rows),
        (1,),
        (sent_to, edges),
        (loc_acc, rand_acc, from_left, from_right, *totals),
        [whole((rows,) + unit)] * 2 + [whole(unit)] * (2 + NGLOB),
        [shape(unit, BF16)] * rows,
        [whole(unit)] * rows,
    )
    kv_done = [kv_back[0]]
    for s in range(1, nh):
        kv_done.append(lax.ppermute(kv_back[s], "head", ring("head", s)))
    grad_keys, grad_values = joined(came_from, kv_done)
    dq_in, grad_keys, grad_values = lax.optimization_barrier((dq_in, grad_keys, grad_values))

    one = (1, BLOCK, features)
    q_back = call(
        partial(finish_q_body, rows),
        (1,),
        (sent_to, owner_mine),
        (dq_loc, dq_in),
        [whole(dq_loc.shape), whole(dq_in.shape)],
        [shape(one, BF16)] * rows,
        [whole(one)] * rows,
    )
    q_done = [q_back[0]]
    for s in range(1, nh):
        q_done.append(lax.ppermute(q_back[s], "head", ring("head", s)))
    [grad_query] = joined(came_from, q_done)
    return grad_query, grad_keys, grad_values


def solution(mesh):
    count, nh = mesh.devices.shape
    fine = Mesh(mesh.devices.reshape(count // NX, NX, nh), ("z", "x", "head"))
    tokens = P(("z", "x", "head"), None)
    return jax.shard_map(
        on_device,
        mesh=fine,
        in_specs=(tokens,) * 4 + (P(),) * 3,
        out_specs=(tokens,) * 3,
        check_vma=False,
    )
```
